32 devices in a mesh: grp: 4 (over z), mem: 8 (over y, x, core).
Axes of the slice: x: 2, y: 2, z: 4, core: 2. Of those that a mesh axis runs over, the one named last changes fastest.
Arguments:
- amplitudes: bfloat16 [8, 2048, 256], P('grp', 'mem'), may hold values from -6 to 6
- integrals: bfloat16 [16, 64, 8192], P('grp', None, 'mem'), may hold values from -0.5 to 0.5
- block_list: int32 [4, 4], replicated, may hold values from 0 to 15, as said below
- block_count: int32 [4], replicated, may hold values from 1 to 4, as said below
- block_slot: int32 [16], replicated, may hold values from 0 to 15, as said below
Outputs:
- residual: float32 [8, 2048, 8192], P('grp', None, 'mem')
The draws below stay inside these ranges and needn't reach their ends.
Inputs may be any that keep to these rules, and one draw needn't show every extreme that they name: `block_list`: each row holds distinct blocks. Of one row's blocks, at most 2 have slots owned by the same grp index, and some row has exactly 2 such among its live positions. `block_count`: some list is full in every draw. `block_slot`: A permutation of the slots.
All inputs are finite; a program needn't handle non-finite values.
Results may differ from the reference program's by a relative error of at most 0.0003.
Values may be sent and summed in bfloat16 or wider, within the bound.
A program may use at most 128 MiB of HBM per device.

```python
import jax
import jax.numpy as jnp
from jax import lax

TILE = 64
NV = 2048
NJ = 4
OCC_GRP = 2
SLOTS = 4
CAP = 2
LISTED = 4
BLOCKS = 16
NI = 8
N_GRP = 4


def permute_each(base_key, count, length):
    many_keys = jax.random.split(base_key, count)
    return jax.vmap(lambda one_key: jax.random.permutation(one_key, length))(many_keys)


def put_first(order, wanted):
    where_at = jnp.argmax((order == wanted).astype(jnp.int32)).astype(jnp.int32)
    first_value = order[0]
    return order.at[where_at].set(first_value).at[0].set(wanted)


def shared_layout(key):
    slot_key = jax.random.fold_in(key, 11)
    block_slot = jax.random.permutation(slot_key, BLOCKS).astype(jnp.int32)
    block_at = jnp.argsort(block_slot, stable=True).astype(jnp.int32)
    owner_order = permute_each(jax.random.fold_in(key, 12), N_GRP, N_GRP).astype(jnp.int32)
    local_full = permute_each(jax.random.fold_in(key, 13), N_GRP * N_GRP, SLOTS).astype(jnp.int32)
    local_full = local_full.reshape(N_GRP, N_GRP, SLOTS)
    slot_low = block_slot[0]
    slot_high = block_slot[BLOCKS - 1]
    owner_order = owner_order.at[0].set(put_first(owner_order[0], slot_low // SLOTS))
    owner_order = owner_order.at[1].set(put_first(owner_order[1], slot_high // SLOTS))
    local_full = local_full.at[0, slot_low // SLOTS].set(put_first(local_full[0, slot_low // SLOTS], slot_low % SLOTS))
    local_full = local_full.at[1, slot_high // SLOTS].set(put_first(local_full[1, slot_high // SLOTS], slot_high % SLOTS))
    local_pick = local_full[:, :, :CAP]
    positions = jnp.arange(LISTED, dtype=jnp.int32)
    owner_pos = owner_order[:, positions // CAP]
    group_rows = jnp.arange(N_GRP, dtype=jnp.int32)[:, None]
    local_pos = local_pick[group_rows, owner_pos, (positions % CAP)[None, :]]
    blocks = block_at[owner_pos * SLOTS + local_pos]
    shuffles = permute_each(jax.random.fold_in(key, 14), N_GRP, LISTED).astype(jnp.int32)
    blocks = jnp.take_along_axis(blocks, shuffles, axis=1)
    return (block_slot, blocks.astype(jnp.int32))


def draw_block_slot(key, part):
    return shared_layout(key)[0]


def draw_block_list(key, part):
    return shared_layout(key)[1]


def draw_block_count(key, part):
    key = jax.random.fold_in(key, 21)
    first_key, second_key = jax.random.split(key)
    divisors = 1 + jax.random.randint(first_key, (N_GRP,), 0, 4)
    counts = LISTED // divisors
    forced = jax.random.randint(second_key, (), 0, N_GRP)
    lowest = (forced + 1) % N_GRP
    rows = jnp.arange(N_GRP)
    counts = jnp.where(rows == lowest, LISTED // 4, counts)
    return jnp.where(rows == forced, LISTED, counts).astype(jnp.int32)


def shard_levels(rng, extent, pieces, low, largest):
    loudness = 1.0
    for position, parts in pieces:
        steps = jax.random.uniform(jax.random.fold_in(jax.random.fold_in(rng, 6), position), (parts,), jnp.float32, low / len(pieces), largest / len(pieces))
        loudness = loudness * jnp.repeat(jnp.exp(steps), extent[position] // parts).reshape((-1,) + (1,) * (len(extent) - 1 - position))
    return loudness


def noise(stream_key, dims, width, reach, pieces=(), kind=jnp.bfloat16):
    values = width * jax.random.normal(stream_key, dims, jnp.float32)
    if pieces:
        values = values * shard_levels(stream_key, dims, pieces, -0.22, 0.18)
    return jnp.clip(values, -reach, reach).astype(kind)


def setup_inputs(seed: int = 0) -> dict:
    splits = jax.random.split(jax.random.key(seed), 6)
    return {
        "amplitudes": noise(splits[0], (NI, NV, LISTED * TILE), 1.0, 6.0, ((0, 4), (1, 8))),
        "integrals": noise(splits[1], (BLOCKS, TILE, NJ * NV), (LISTED * TILE // 2) ** -0.5, 0.5, ((0, 4), (2, 8))),
        "block_list": draw_block_list(jax.random.fold_in(splits[5], 71), 0),
        "block_count": draw_block_count(jax.random.fold_in(splits[5], 71), 0),
        "block_slot": draw_block_slot(jax.random.fold_in(splits[5], 71), 0),
    }


def reference(amplitudes, integrals, block_list, block_count, block_slot):
    slot_table = block_slot[block_list]
    is_live = jnp.arange(LISTED, dtype=jnp.int32)[None, :] < block_count[:, None]
    rows_left = amplitudes.reshape(N_GRP, OCC_GRP * NV, LISTED * TILE)

    def one_group(packed):
        left_rows, slots, live_row = packed
        chosen = integrals[slots] * live_row[:, None, None].astype(integrals.dtype)
        return jnp.dot(left_rows, chosen.reshape(LISTED * TILE, NJ * NV), preferred_element_type=jnp.float32)

    result = lax.map(one_group, (rows_left, slot_table, is_live))
    return result.reshape(N_GRP * OCC_GRP, NV, NJ * NV)
```

```python
import functools

import jax
import jax.numpy as jnp
from jax import lax
from jax.experimental import pallas as pl
from jax.experimental.pallas import tpu as pltpu
from jax.sharding import PartitionSpec as P

CAP = 2
MESH = pl.DeviceIdType.MESH
CHUNKS = 2


def exchange_kernel(
    groups, tiles_ref, list_ref, count_ref, slot_ref, amp_ref, all_ref, recv_ref,
    stage, own_sem, z_send, z_recv, a_send, a_recv,
):
    z = lax.axis_index("grp")
    m = lax.axis_index("mem")
    c, x, y = m % 2, (m // 2) % 2, m // 4
    sib = (y * 2 + x) * 2 + (1 - c)
    xn = (y * 2 + (1 - x)) * 2 + c
    yn = ((1 - y) * 2 + x) * 2 + c
    dg = ((1 - y) * 2 + (1 - x)) * 2 + c
    slots = tiles_ref.shape[0]
    listed = list_ref.shape[1]
    occ, rows = amp_ref.shape[0], amp_ref.shape[1]
    part = rows // CHUNKS
    pieces = [(i, h) for h in range(CHUNKS) for i in range(occ)]

    barrier = pltpu.get_barrier_semaphore()
    near = [(z, sib), (z, xn), (z, yn)]
    far = [(lax.rem(z + d, groups), m) for d in range(1, groups)]
    for device in near + far:
        pl.semaphore_signal(barrier, inc=1, device_id=device, device_id_type=MESH)

    def block(owner, piece):
        i, h = piece
        return all_ref.at[i, pl.ds(pl.multiple_of(owner * rows + h * part, 16), part)]

    own = pltpu.make_async_copy(
        amp_ref, all_ref.at[:, pl.ds(pl.multiple_of(m * rows, 16), rows)], own_sem
    )
    own.start()

    for d in range(1, groups):
        r = lax.rem(z + d, groups)
        seen = jnp.int32(0)
        first = jnp.int32(0)
        second = jnp.int32(0)
        for l in range(listed):
            slot = slot_ref[list_ref[r, l]]
            hit = (slot // slots == z) & (l < count_ref[r])
            local = slot % slots
            first = jnp.where(hit & (seen == 0), local, first)
            second = jnp.where(hit & (seen == 1), local, second)
            seen = seen + hit.astype(jnp.int32)
        stage[(d - 1) * CAP] = tiles_ref[first]
        stage[(d - 1) * CAP + 1] = tiles_ref[second]
    pl.semaphore_wait(barrier, len(near) + len(far))

    copies = []
    for d in (2, 3, 1) if groups == 4 else range(1, groups):
        r = lax.rem(z + d, groups)
        for k in range(CAP):
            index = (d - 1) * CAP + k
            copy = pltpu.make_async_remote_copy(
                stage.at[index], recv_ref.at[z * CAP + k],
                z_send.at[index], z_recv.at[index],
                device_id=(r, m), device_id_type=MESH,
            )
            copies.append(copy)

    def send(kind, k, source, owner, target):
        copy = pltpu.make_async_remote_copy(
            source, block(owner, pieces[k]),
            a_send.at[kind, k], a_recv.at[kind, k],
            device_id=(z, target), device_id_type=MESH,
        )
        copy.start()
        copies.append(copy)
        return copy

    count = len(pieces)
    from_x, from_y, from_dg = [], [], []
    mine = [amp_ref.at[i, pl.ds(h * part, part)] for i, h in pieces]
    for k in range(count):
        from_x.append(send(0, k, mine[k], m, xn))
        from_y.append(send(1, k, mine[k], m, yn))
        if k == 0:
            for copy in copies[: (groups - 1) * CAP]:
                copy.start()
    for k in range(count):
        send(2, k, mine[k], m, sib)
    arrived = []
    for k in range(count):
        from_x[k].wait_recv()
        if k % 2 == 0:
            from_dg.append(send(3, k, block(xn, pieces[k]), xn, yn))
        send(4, k, block(xn, pieces[k]), xn, sib)
        from_y[k].wait_recv()
        if k % 2 == 1:
            from_dg.append(send(3, k, block(yn, pieces[k]), yn, xn))
        send(5, k, block(yn, pieces[k]), yn, sib)
    for k in range(count):
        from_dg[k].wait_recv()
        send(6, k, block(dg, pieces[k]), dg, sib)
    waited = {id(copy) for copy in from_x + from_y + from_dg}
    own.wait()
    for copy in copies:
        if id(copy) not in waited:
            copy.wait_recv()
    for copy in copies:
        copy.wait_send()


def exchange(amplitudes, integrals, block_list, block_count, block_slot):
    groups, members = lax.axis_size("grp"), lax.axis_size("mem")
    occ, rows, depth = amplitudes.shape
    tile_rows, columns = integrals.shape[1:]
    count = occ * CHUNKS
    smem = pl.BlockSpec(memory_space=pltpu.SMEM)
    return pl.pallas_call(
        functools.partial(exchange_kernel, groups),
        name="exchange",
        out_shape=(
            jax.ShapeDtypeStruct((occ, rows * members, depth), amplitudes.dtype),
            jax.ShapeDtypeStruct((groups * CAP, tile_rows, columns), integrals.dtype),
        ),
        in_specs=[pl.BlockSpec(memory_space=pltpu.VMEM), smem, smem, smem,
                  pl.BlockSpec(memory_space=pl.ANY)],
        out_specs=(pl.BlockSpec(memory_space=pl.ANY), pl.BlockSpec(memory_space=pl.ANY)),
        scratch_shapes=[
            pltpu.VMEM(((groups - 1) * CAP, tile_rows, columns), integrals.dtype),
            pltpu.SemaphoreType.DMA,
            pltpu.SemaphoreType.DMA(((groups - 1) * CAP,)),
            pltpu.SemaphoreType.DMA(((groups - 1) * CAP,)),
            pltpu.SemaphoreType.DMA((7, count)),
            pltpu.SemaphoreType.DMA((7, count)),
        ],
        compiler_params=pltpu.CompilerParams(
            collective_id=0, has_side_effects=True, vmem_limit_bytes=32 * 2**20
        ),
    )(integrals, block_list, block_count, block_slot, amplitudes)


def product_kernel(
    own_ref, list_ref, count_ref, slot_ref, amp_ref, tiles_ref, recv_ref, out_ref,
    weights, sems,
):
    slots, tile_rows = tiles_ref.shape[0], tiles_ref.shape[1]
    listed = list_ref.shape[1]
    z = own_ref[0]

    @pl.when((pl.program_id(0) == 0) & (pl.program_id(1) == 0))
    def _():
        slot = [slot_ref[list_ref[z, l]] for l in range(listed)]
        live = [l < count_ref[z] for l in range(listed)]
        for l in range(listed):
            owner = slot[l] // slots
            rank = jnp.int32(0)
            for e in range(l):
                rank = rank + (slot[e] // slots == owner).astype(jnp.int32)
            part = weights.at[pl.ds(l * tile_rows, tile_rows)]

            @pl.when(live[l] & (owner == z))
            def _():
                pltpu.make_async_copy(
                    tiles_ref.at[slot[l] % slots], part, sems.at[l]
                ).start()

            @pl.when(live[l] & (owner != z))
            def _():
                pltpu.make_async_copy(
                    recv_ref.at[owner * CAP + rank], part, sems.at[l]
                ).start()

            @pl.when(jnp.logical_not(live[l]))
            def _():
                part[...] = jnp.zeros(part.shape, part.dtype)

        for l in range(listed):
            part = weights.at[pl.ds(l * tile_rows, tile_rows)]

            @pl.when(live[l])
            def _():
                pltpu.make_async_copy(tiles_ref.at[0], part, sems.at[l]).wait()

    out_ref[0] = jnp.dot(
        amp_ref[0], weights[...], preferred_element_type=jnp.float32
    )


def product(amplitudes, integrals, received, block_list, block_count, block_slot):
    occ, rows, depth = amplitudes.shape
    tile_rows, columns = integrals.shape[1:]
    listed = block_list.shape[1]
    step = 256
    own = lax.axis_index("grp").astype(jnp.int32).reshape(1)
    hbm = pl.BlockSpec(memory_space=pl.ANY)
    return pl.pallas_call(
        product_kernel,
        name="product",
        out_shape=jax.ShapeDtypeStruct((occ, rows, columns), jnp.float32),
        grid_spec=pltpu.PrefetchScalarGridSpec(
            num_scalar_prefetch=4,
            grid=(occ, rows // step),
            in_specs=[pl.BlockSpec((1, step, depth), lambda i, r, *_: (i, r, 0)), hbm, hbm],
            out_specs=pl.BlockSpec((1, step, columns), lambda i, r, *_: (i, r, 0)),
            scratch_shapes=[
                pltpu.VMEM((listed * tile_rows, columns), integrals.dtype),
                pltpu.SemaphoreType.DMA((listed,)),
            ],
        ),
        compiler_params=pltpu.CompilerParams(vmem_limit_bytes=32 * 2**20),
    )(own, block_list, block_count, block_slot, amplitudes, integrals, received)


def gathered_path(amplitudes, integrals, block_list, block_count, block_slot):
    groups = lax.axis_size("grp")
    me = lax.axis_index("grp")
    listed = block_list.shape[1]
    slots, tile_rows, columns = integrals.shape
    table = block_slot[block_list]
    owner, local = table // slots, table % slots
    positions = jnp.arange(listed, dtype=jnp.int32)
    same = owner[:, :, None] == owner[:, None, :]
    same = same & (positions[None, None, :] < positions[None, :, None])
    rank = jnp.sum(same.astype(jnp.int32), axis=2)
    live = positions[None, :] < block_count[:, None]
    pick = (live & (owner == me))[:, None, :] & (
        rank[:, None, :] == jnp.arange(CAP, dtype=jnp.int32)[None, :, None]
    )
    sent = jnp.sum(jnp.where(pick, local[:, None, :], 0), axis=2)
    outgoing = integrals[sent.reshape(-1)].reshape(groups, CAP, tile_rows, columns)
    incoming = lax.all_to_all(outgoing, "grp", split_axis=0, concat_axis=0, tiled=True)
    incoming = incoming.reshape(groups * CAP, tile_rows, columns)
    return lax.all_gather(amplitudes, "mem", axis=1, tiled=True), incoming


def per_device(by_kernel, amplitudes, integrals, block_list, block_count, block_slot):
    move = exchange if by_kernel else gathered_path
    rows, received = move(amplitudes, integrals, block_list, block_count, block_slot)
    return product(rows, integrals, received, block_list, block_count, block_slot)


def solution(mesh):
    in_specs = (P("grp", "mem", None), P("grp", None, "mem"), P(), P(), P())
    out_specs = P("grp", None, "mem")
    by_kernel = mesh.shape["mem"] == 8 and mesh.shape["grp"] == 4
    return jax.shard_map(
        functools.partial(per_device, by_kernel), mesh=mesh,
        in_specs=in_specs, out_specs=out_specs, check_vma=False,
    )
```

```python
import functools

import jax
import jax.numpy as jnp
from jax import lax
from jax.experimental import pallas as pl
from jax.experimental.pallas import tpu as pltpu
from jax.sharding import PartitionSpec as P

CAP = 2
MESH = pl.DeviceIdType.MESH
CHUNKS = 2


def load_tables(sources, targets, sem):
    copies = [
        pltpu.make_async_copy(source, target, sem.at[k])
        for k, (source, target) in enumerate(zip(sources, targets))
    ]
    for copy in copies:
        copy.start()
    return copies


def table_scratch(block_list, block_count, block_slot):
    tables = (block_list, block_count, block_slot)
    return [pltpu.SMEM(t.shape, t.dtype) for t in tables] + [pltpu.SemaphoreType.DMA((3,))]


def exchange_kernel(
    groups, tiles_ref, list_hbm, count_hbm, slot_hbm, amp_ref, all_ref, recv_ref,
    list_ref, count_ref, slot_ref, table_sem, stage, own_sem, z_send, z_recv, a_send, a_recv,
):
    z = lax.axis_index("grp")
    m = lax.axis_index("mem")
    c, x, y = m % 2, (m // 2) % 2, m // 4
    sib = (y * 2 + x) * 2 + (1 - c)
    xn = (y * 2 + (1 - x)) * 2 + c
    yn = ((1 - y) * 2 + x) * 2 + c
    dg = ((1 - y) * 2 + (1 - x)) * 2 + c
    slots = tiles_ref.shape[0]
    listed = list_ref.shape[1]
    occ, rows = amp_ref.shape[0], amp_ref.shape[1]
    part = rows // CHUNKS
    pieces = [(i, h) for h in range(CHUNKS) for i in range(occ)]

    tables = load_tables(
        (list_hbm, count_hbm, slot_hbm), (list_ref, count_ref, slot_ref), table_sem
    )
    barrier = pltpu.get_barrier_semaphore()
    near = [(z, sib), (z, xn), (z, yn)]
    far = [(lax.rem(z + d, groups), m) for d in range(1, groups)]
    for device in near + far:
        pl.semaphore_signal(barrier, inc=1, device_id=device, device_id_type=MESH)

    def block(owner, piece):
        i, h = piece
        return all_ref.at[i, pl.ds(pl.multiple_of(owner * rows + h * part, 16), part)]

    own = pltpu.make_async_copy(
        amp_ref, all_ref.at[:, pl.ds(pl.multiple_of(m * rows, 16), rows)], own_sem
    )
    own.start()
    for copy in tables:
        copy.wait()

    for d in range(1, groups):
        r = lax.rem(z + d, groups)
        seen = jnp.int32(0)
        first = jnp.int32(0)
        second = jnp.int32(0)
        for l in range(listed):
            slot = slot_ref[list_ref[r, l]]
            hit = (slot // slots == z) & (l < count_ref[r])
            local = slot % slots
            first = jnp.where(hit & (seen == 0), local, first)
            second = jnp.where(hit & (seen == 1), local, second)
            seen = seen + hit.astype(jnp.int32)
        stage[(d - 1) * CAP] = tiles_ref[first]
        stage[(d - 1) * CAP + 1] = tiles_ref[second]
    pl.semaphore_wait(barrier, len(near) + len(far))

    copies = []
    for d in (2, 3, 1) if groups == 4 else range(1, groups):
        r = lax.rem(z + d, groups)
        for k in range(CAP):
            index = (d - 1) * CAP + k
            copy = pltpu.make_async_remote_copy(
                stage.at[index], recv_ref.at[z * CAP + k],
                z_send.at[index], z_recv.at[index],
                device_id=(r, m), device_id_type=MESH,
            )
            copies.append(copy)

    def send(kind, k, source, owner, target):
        copy = pltpu.make_async_remote_copy(
            source, block(owner, pieces[k]),
            a_send.at[kind, k], a_recv.at[kind, k],
            device_id=(z, target), device_id_type=MESH,
        )
        copy.start()
        copies.append(copy)
        return copy

    count = len(pieces)
    from_x, from_y, from_dg = [], [], []
    mine = [amp_ref.at[i, pl.ds(h * part, part)] for i, h in pieces]
    for k in range(count):
        from_x.append(send(0, k, mine[k], m, xn))
        from_y.append(send(1, k, mine[k], m, yn))
        if k == 0:
            for copy in copies[: (groups - 1) * CAP]:
                copy.start()
    for k in range(count):
        send(2, k, mine[k], m, sib)
    arrived = []
    for k in range(count):
        from_x[k].wait_recv()
        if k % 2 == 0:
            from_dg.append(send(3, k, block(xn, pieces[k]), xn, yn))
        send(4, k, block(xn, pieces[k]), xn, sib)
        from_y[k].wait_recv()
        if k % 2 == 1:
            from_dg.append(send(3, k, block(yn, pieces[k]), yn, xn))
        send(5, k, block(yn, pieces[k]), yn, sib)
    for k in range(count):
        from_dg[k].wait_recv()
        send(6, k, block(dg, pieces[k]), dg, sib)
    waited = {id(copy) for copy in from_x + from_y + from_dg}
    own.wait()
    for copy in copies:
        if id(copy) not in waited:
            copy.wait_recv()
    for copy in copies:
        copy.wait_send()


def exchange(amplitudes, integrals, block_list, block_count, block_slot):
    groups, members = lax.axis_size("grp"), lax.axis_size("mem")
    occ, rows, depth = amplitudes.shape
    tile_rows, columns = integrals.shape[1:]
    count = occ * CHUNKS
    hbm = pl.BlockSpec(memory_space=pl.ANY)
    return pl.pallas_call(
        functools.partial(exchange_kernel, groups),
        name="exchange",
        out_shape=(
            jax.ShapeDtypeStruct((occ, rows * members, depth), amplitudes.dtype),
            jax.ShapeDtypeStruct((groups * CAP, tile_rows, columns), integrals.dtype),
        ),
        in_specs=[pl.BlockSpec(memory_space=pltpu.VMEM)] + [hbm] * 4,
        out_specs=(hbm, hbm),
        scratch_shapes=table_scratch(block_list, block_count, block_slot) + [
            pltpu.VMEM(((groups - 1) * CAP, tile_rows, columns), integrals.dtype),
            pltpu.SemaphoreType.DMA,
            pltpu.SemaphoreType.DMA(((groups - 1) * CAP,)),
            pltpu.SemaphoreType.DMA(((groups - 1) * CAP,)),
            pltpu.SemaphoreType.DMA((7, count)),
            pltpu.SemaphoreType.DMA((7, count)),
        ],
        compiler_params=pltpu.CompilerParams(
            collective_id=0, has_side_effects=True, vmem_limit_bytes=32 * 2**20
        ),
    )(integrals, block_list, block_count, block_slot, amplitudes)


def product_kernel(
    step, list_hbm, count_hbm, slot_hbm, amp_hbm, tiles_ref, recv_ref, out_ref,
    list_ref, count_ref, slot_ref, table_sem, amp, weights, made, sems, amp_sem, out_sem,
):
    occ, rows, depth = amp_hbm.shape
    slots, tile_rows = tiles_ref.shape[0], tiles_ref.shape[1]
    listed = list_ref.shape[1]
    z = lax.axis_index("grp")
    buffers = made.shape[0]
    per = rows // step
    tables = load_tables(
        (list_hbm, count_hbm, slot_hbm), (list_ref, count_ref, slot_ref), table_sem
    )
    held = amp.shape[0]

    def fetch(t):
        return pltpu.make_async_copy(
            amp_hbm.at[t // per, pl.ds(pl.multiple_of((t % per) * step, 16), step)],
            amp.at[t % held], amp_sem.at[t % held],
        )

    for t in range(held):
        fetch(t).start()
    for copy in tables:
        copy.wait()

    def pick(l):
        return weights.at[pl.ds(pl.multiple_of(l * tile_rows, 16), tile_rows)]

    @pl.loop(0, listed)
    def _(l):
        slot = slot_ref[list_ref[z, l]]
        owner = slot // slots
        live = l < count_ref[z]

        def count_same(e, rank):
            return rank + (slot_ref[list_ref[z, e]] // slots == owner).astype(jnp.int32)

        rank = lax.fori_loop(0, l, count_same, jnp.int32(0))

        @pl.when(live & (owner == z))
        def _():
            pltpu.make_async_copy(tiles_ref.at[slot % slots], pick(l), sems.at[l]).start()

        @pl.when(live & (owner != z))
        def _():
            pltpu.make_async_copy(
                recv_ref.at[owner * CAP + rank], pick(l), sems.at[l]
            ).start()

        @pl.when(jnp.logical_not(live))
        def _():
            part = pick(l)
            part[...] = jnp.zeros(part.shape, part.dtype)

    @pl.loop(0, listed)
    def _(l):
        @pl.when(l < count_ref[z])
        def _():
            pltpu.make_async_copy(tiles_ref.at[0], pick(l), sems.at[l]).wait()

    def put(t):
        return pltpu.make_async_copy(
            made.at[t % buffers],
            out_ref.at[t // per, pl.ds(pl.multiple_of((t % per) * step, 8), step)],
            out_sem.at[t % buffers],
        )

    total = occ * per

    @pl.loop(0, total)
    def _(t):
        fetch(t).wait()

        @pl.when(t >= buffers)
        def _():
            put(t - buffers).wait()

        made[t % buffers] = jnp.dot(
            amp[t % held], weights[...], preferred_element_type=jnp.float32
        )
        put(t).start()

        @pl.when(t + held < total)
        def _():
            fetch(t + held).start()

    @pl.loop(total - buffers, total)
    def _(t):
        put(t).wait()


def product(amplitudes, integrals, received, block_list, block_count, block_slot):
    occ, rows, depth = amplitudes.shape
    tile_rows, columns = integrals.shape[1:]
    listed = block_list.shape[1]
    step = 128
    buffers = min(8, occ * rows // step)
    hbm = pl.BlockSpec(memory_space=pl.ANY)
    return pl.pallas_call(
        functools.partial(product_kernel, step),
        name="product",
        out_shape=jax.ShapeDtypeStruct((occ, rows, columns), jnp.float32),
        in_specs=[hbm] * 6,
        out_specs=hbm,
        scratch_shapes=table_scratch(block_list, block_count, block_slot) + [
            pltpu.VMEM((buffers, step, depth), amplitudes.dtype),
            pltpu.VMEM((listed * tile_rows, columns), integrals.dtype),
            pltpu.VMEM((buffers, step, columns), jnp.float32),
            pltpu.SemaphoreType.DMA((listed,)),
            pltpu.SemaphoreType.DMA((buffers,)),
            pltpu.SemaphoreType.DMA((buffers,)),
        ],
        compiler_params=pltpu.CompilerParams(vmem_limit_bytes=40 * 2**20),
    )(block_list, block_count, block_slot, amplitudes, integrals, received)


def gathered_path(amplitudes, integrals, block_list, block_count, block_slot):
    groups = lax.axis_size("grp")
    me = lax.axis_index("grp")
    listed = block_list.shape[1]
    slots, tile_rows, columns = integrals.shape
    table = block_slot[block_list]
    owner, local = table // slots, table % slots
    positions = jnp.arange(listed, dtype=jnp.int32)
    same = owner[:, :, None] == owner[:, None, :]
    same = same & (positions[None, None, :] < positions[None, :, None])
    rank = jnp.sum(same.astype(jnp.int32), axis=2)
    live = positions[None, :] < block_count[:, None]
    pick = (live & (owner == me))[:, None, :] & (
        rank[:, None, :] == jnp.arange(CAP, dtype=jnp.int32)[None, :, None]
    )
    sent = jnp.sum(jnp.where(pick, local[:, None, :], 0), axis=2)
    outgoing = integrals[sent.reshape(-1)].reshape(groups, CAP, tile_rows, columns)
    incoming = lax.all_to_all(outgoing, "grp", split_axis=0, concat_axis=0, tiled=True)
    incoming = incoming.reshape(groups * CAP, tile_rows, columns)
    return lax.all_gather(amplitudes, "mem", axis=1, tiled=True), incoming


def per_device(by_kernel, amplitudes, integrals, block_list, block_count, block_slot):
    move = exchange if by_kernel else gathered_path
    rows, received = move(amplitudes, integrals, block_list, block_count, block_slot)
    return product(rows, integrals, received, block_list, block_count, block_slot)


def solution(mesh):
    in_specs = (P("grp", "mem", None), P("grp", None, "mem"), P(), P(), P())
    out_specs = P("grp", None, "mem")
    by_kernel = mesh.shape["mem"] == 8 and mesh.shape["grp"] == 4
    return jax.shard_map(
        functools.partial(per_device, by_kernel), mesh=mesh,
        in_specs=in_specs, out_specs=out_specs, check_vma=False,
    )
```

```python
import functools

import jax
import jax.numpy as jnp
from jax import lax
from jax.experimental import pallas as pl
from jax.experimental.pallas import tpu as pltpu
from jax.sharding import PartitionSpec as P

CAP = 2
MESH = pl.DeviceIdType.MESH
CHUNKS = 2


def load_tables(sources, targets, sem):
    copies = [
        pltpu.make_async_copy(source, target, sem.at[k])
        for k, (source, target) in enumerate(zip(sources, targets))
    ]
    for copy in copies:
        copy.start()
    return copies


def table_scratch(block_list, block_count, block_slot):
    tables = (block_list, block_count, block_slot)
    return [pltpu.SMEM(t.shape, t.dtype) for t in tables] + [pltpu.SemaphoreType.DMA((3,))]


def exchange_kernel(
    groups, tiles_ref, list_hbm, count_hbm, slot_hbm, amp_ref, all_ref, recv_ref,
    list_ref, count_ref, slot_ref, table_sem, stage, own_sem, z_send, z_recv, a_send, a_recv,
):
    z = lax.axis_index("grp")
    m = lax.axis_index("mem")
    c, x, y = m % 2, (m // 2) % 2, m // 4
    sib = (y * 2 + x) * 2 + (1 - c)
    xn = (y * 2 + (1 - x)) * 2 + c
    yn = ((1 - y) * 2 + x) * 2 + c
    dg = ((1 - y) * 2 + (1 - x)) * 2 + c
    slots = tiles_ref.shape[0]
    listed = list_ref.shape[1]
    occ, rows = amp_ref.shape[0], amp_ref.shape[1]
    part = rows // CHUNKS
    pieces = [(i, h) for h in range(CHUNKS) for i in range(occ)]

    tables = load_tables(
        (list_hbm, count_hbm, slot_hbm), (list_ref, count_ref, slot_ref), table_sem
    )
    barrier = pltpu.get_barrier_semaphore()
    near = [(z, sib), (z, xn), (z, yn)]
    far = [(lax.rem(z + d, groups), m) for d in range(1, groups)]
    for device in near + far:
        pl.semaphore_signal(barrier, inc=1, device_id=device, device_id_type=MESH)

    def block(owner, piece):
        i, h = piece
        return all_ref.at[i, pl.ds(pl.multiple_of(owner * rows + h * part, 16), part)]

    own = pltpu.make_async_copy(
        amp_ref, all_ref.at[:, pl.ds(pl.multiple_of(m * rows, 16), rows)], own_sem
    )
    own.start()
    for copy in tables:
        copy.wait()

    for d in range(1, groups):
        r = lax.rem(z + d, groups)
        seen = jnp.int32(0)
        first = jnp.int32(0)
        second = jnp.int32(0)
        for l in range(listed):
            slot = slot_ref[list_ref[r, l]]
            hit = (slot // slots == z) & (l < count_ref[r])
            local = slot % slots
            first = jnp.where(hit & (seen == 0), local, first)
            second = jnp.where(hit & (seen == 1), local, second)
            seen = seen + hit.astype(jnp.int32)
        stage[(d - 1) * CAP] = tiles_ref[first]
        stage[(d - 1) * CAP + 1] = tiles_ref[second]
    pl.semaphore_wait(barrier, len(near) + len(far))

    copies = []
    for d in (2, 3, 1) if groups == 4 else range(1, groups):
        r = lax.rem(z + d, groups)
        for k in range(CAP):
            index = (d - 1) * CAP + k
            copy = pltpu.make_async_remote_copy(
                stage.at[index], recv_ref.at[z * CAP + k],
                z_send.at[index], z_recv.at[index],
                device_id=(r, m), device_id_type=MESH,
            )
            copies.append(copy)

    def send(kind, k, source, owner, target):
        copy = pltpu.make_async_remote_copy(
            source, block(owner, pieces[k]),
            a_send.at[kind, k], a_recv.at[kind, k],
            device_id=(z, target), device_id_type=MESH,
        )
        copy.start()
        copies.append(copy)
        return copy

    count = len(pieces)
    from_x, from_y, from_dg = [], [], []
    mine = [amp_ref.at[i, pl.ds(h * part, part)] for i, h in pieces]
    for k in range(count):
        from_x.append(send(0, k, mine[k], m, xn))
        from_y.append(send(1, k, mine[k], m, yn))
        if k == 0:
            for copy in copies[: (groups - 1) * CAP]:
                copy.start()
    for k in range(count):
        send(2, k, mine[k], m, sib)
    arrived = []
    for k in range(count):
        from_x[k].wait_recv()
        if k % 2 == 0:
            from_dg.append(send(3, k, block(xn, pieces[k]), xn, yn))
        send(4, k, block(xn, pieces[k]), xn, sib)
        from_y[k].wait_recv()
        if k % 2 == 1:
            from_dg.append(send(3, k, block(yn, pieces[k]), yn, xn))
        send(5, k, block(yn, pieces[k]), yn, sib)
    for k in range(count):
        from_dg[k].wait_recv()
        send(6, k, block(dg, pieces[k]), dg, sib)
    waited = {id(copy) for copy in from_x + from_y + from_dg}
    own.wait()
    for copy in copies:
        if id(copy) not in waited:
            copy.wait_recv()
    for copy in copies:
        copy.wait_send()


def exchange(amplitudes, integrals, block_list, block_count, block_slot):
    groups, members = lax.axis_size("grp"), lax.axis_size("mem")
    occ, rows, depth = amplitudes.shape
    tile_rows, columns = integrals.shape[1:]
    count = occ * CHUNKS
    hbm = pl.BlockSpec(memory_space=pltpu.HBM)
    return pl.pallas_call(
        functools.partial(exchange_kernel, groups),
        name="exchange",
        out_shape=(
            jax.ShapeDtypeStruct((occ, rows * members, depth), amplitudes.dtype),
            jax.ShapeDtypeStruct((groups * CAP, tile_rows, columns), integrals.dtype),
        ),
        in_specs=[pl.BlockSpec(memory_space=pltpu.VMEM)] + [hbm] * 4,
        out_specs=(hbm, hbm),
        scratch_shapes=table_scratch(block_list, block_count, block_slot) + [
            pltpu.VMEM(((groups - 1) * CAP, tile_rows, columns), integrals.dtype),
            pltpu.SemaphoreType.DMA,
            pltpu.SemaphoreType.DMA(((groups - 1) * CAP,)),
            pltpu.SemaphoreType.DMA(((groups - 1) * CAP,)),
            pltpu.SemaphoreType.DMA((7, count)),
            pltpu.SemaphoreType.DMA((7, count)),
        ],
        compiler_params=pltpu.CompilerParams(
            collective_id=0, has_side_effects=True, vmem_limit_bytes=32 * 2**20
        ),
    )(integrals, block_list, block_count, block_slot, amplitudes)


def product_kernel(
    step, list_hbm, count_hbm, slot_hbm, amp_hbm, tiles_ref, recv_ref, out_ref,
    list_ref, count_ref, slot_ref, table_sem, amp, weights, made, sems, amp_sem, out_sem,
):
    occ, rows, depth = amp_hbm.shape
    slots, tile_rows = tiles_ref.shape[0], tiles_ref.shape[1]
    listed = list_ref.shape[1]
    z = lax.axis_index("grp")
    buffers = made.shape[0]
    per = rows // step
    tables = load_tables(
        (list_hbm, count_hbm, slot_hbm), (list_ref, count_ref, slot_ref), table_sem
    )
    held = amp.shape[0]

    def fetch(t):
        return pltpu.make_async_copy(
            amp_hbm.at[t // per, pl.ds((t % per) * step, step)],
            amp.at[t % held], amp_sem.at[t % held],
        )

    for t in range(held):
        fetch(t).start()
    for copy in tables:
        copy.wait()

    def pick(l):
        return weights.at[pl.ds(pl.multiple_of(l * tile_rows, 16), tile_rows)]

    @pl.loop(0, listed)
    def _(l):
        slot = slot_ref[list_ref[z, l]]
        owner = slot // slots
        live = l < count_ref[z]

        def count_same(e, rank):
            return rank + (slot_ref[list_ref[z, e]] // slots == owner).astype(jnp.int32)

        rank = lax.fori_loop(0, l, count_same, jnp.int32(0))

        @pl.when(live & (owner == z))
        def _():
            pltpu.make_async_copy(tiles_ref.at[slot % slots], pick(l), sems.at[l]).start()

        @pl.when(live & (owner != z))
        def _():
            pltpu.make_async_copy(
                recv_ref.at[owner * CAP + rank], pick(l), sems.at[l]
            ).start()

        @pl.when(jnp.logical_not(live))
        def _():
            part = pick(l)
            part[...] = jnp.zeros(part.shape, part.dtype)

    @pl.loop(0, listed)
    def _(l):
        @pl.when(l < count_ref[z])
        def _():
            pltpu.make_async_copy(tiles_ref.at[0], pick(l), sems.at[l]).wait()

    def put(t):
        return pltpu.make_async_copy(
            made.at[t % buffers],
            out_ref.at[t // per, pl.ds((t % per) * step, step)],
            out_sem.at[t % buffers],
        )

    total = occ * per
    for t in range(total):
        fetch(t).wait()
        if t >= buffers:
            put(t - buffers).wait()
        made[t % buffers] = jnp.dot(
            amp[t % held], weights[...], preferred_element_type=jnp.float32
        )
        put(t).start()
        if t + held < total:
            fetch(t + held).start()
    for t in range(total - buffers, total):
        put(t).wait()


def product(amplitudes, integrals, received, block_list, block_count, block_slot):
    occ, rows, depth = amplitudes.shape
    tile_rows, columns = integrals.shape[1:]
    listed = block_list.shape[1]
    step = 256
    buffers = min(8, occ * rows // step)
    hbm = pl.BlockSpec(memory_space=pltpu.HBM)
    return pl.pallas_call(
        functools.partial(product_kernel, step),
        name="product",
        out_shape=jax.ShapeDtypeStruct((occ, rows, columns), jnp.float32),
        in_specs=[hbm] * 6,
        out_specs=hbm,
        scratch_shapes=table_scratch(block_list, block_count, block_slot) + [
            pltpu.VMEM((buffers, step, depth), amplitudes.dtype),
            pltpu.VMEM((listed * tile_rows, columns), integrals.dtype),
            pltpu.VMEM((buffers, step, columns), jnp.float32),
            pltpu.SemaphoreType.DMA((listed,)),
            pltpu.SemaphoreType.DMA((buffers,)),
            pltpu.SemaphoreType.DMA((buffers,)),
        ],
        compiler_params=pltpu.CompilerParams(vmem_limit_bytes=40 * 2**20),
    )(block_list, block_count, block_slot, amplitudes, integrals, received)


def gathered_path(amplitudes, integrals, block_list, block_count, block_slot):
    groups = lax.axis_size("grp")
    me = lax.axis_index("grp")
    listed = block_list.shape[1]
    slots, tile_rows, columns = integrals.shape
    table = block_slot[block_list]
    owner, local = table // slots, table % slots
    positions = jnp.arange(listed, dtype=jnp.int32)
    same = owner[:, :, None] == owner[:, None, :]
    same = same & (positions[None, None, :] < positions[None, :, None])
    rank = jnp.sum(same.astype(jnp.int32), axis=2)
    live = positions[None, :] < block_count[:, None]
    pick = (live & (owner == me))[:, None, :] & (
        rank[:, None, :] == jnp.arange(CAP, dtype=jnp.int32)[None, :, None]
    )
    sent = jnp.sum(jnp.where(pick, local[:, None, :], 0), axis=2)
    outgoing = integrals[sent.reshape(-1)].reshape(groups, CAP, tile_rows, columns)
    incoming = lax.all_to_all(outgoing, "grp", split_axis=0, concat_axis=0, tiled=True)
    incoming = incoming.reshape(groups * CAP, tile_rows, columns)
    return lax.all_gather(amplitudes, "mem", axis=1, tiled=True), incoming


def per_device(by_kernel, amplitudes, integrals, block_list, block_count, block_slot):
    move = exchange if by_kernel else gathered_path
    rows, received = move(amplitudes, integrals, block_list, block_count, block_slot)
    return product(rows, integrals, received, block_list, block_count, block_slot)


def solution(mesh):
    in_specs = (P("grp", "mem", None), P("grp", None, "mem"), P(), P(), P())
    out_specs = P("grp", None, "mem")
    by_kernel = mesh.shape["mem"] == 8 and mesh.shape["grp"] == 4
    return jax.shard_map(
        functools.partial(per_device, by_kernel), mesh=mesh,
        in_specs=in_specs, out_specs=out_specs, check_vma=False,
    )
```

```python
import functools

import jax
import jax.numpy as jnp
from jax import lax
from jax.experimental import pallas as pl
from jax.experimental.pallas import tpu as pltpu
from jax.sharding import PartitionSpec as P

CAP = 2
MESH = pl.DeviceIdType.MESH
CHUNKS = 2
PIECES = 2
LEVELS = (2, 3, 4, 5)
VMEM_BYTES = 60 * 2**20


def load_tables(sources, targets, sem):
    copies = [
        pltpu.make_async_copy(source, target, sem.at[k])
        for k, (source, target) in enumerate(zip(sources, targets))
    ]
    for copy in copies:
        copy.start()
    return copies


def table_scratch(block_list, block_count, block_slot):
    tables = (block_list, block_count, block_slot)
    return [pltpu.SMEM(t.shape, t.dtype) for t in tables] + [pltpu.SemaphoreType.DMA((3,))]


def most_flows(groups, listed):
    return max((groups - 1 - k) * min(listed, CAP * (k + 1)) for k in range(groups - 1))


def plan_kernel(
    groups, slots, most, list_hbm, count_hbm, slot_hbm, plan_ref, level_ref,
    list_ref, count_ref, slot_ref, table_sem, colour, free, top, low,
):
    listed = list_hbm.shape[1]
    for copy in load_tables(
        (list_hbm, count_hbm, slot_hbm), (list_ref, count_ref, slot_ref), table_sem
    ):
        copy.wait()
    owner, local, live = {}, {}, {}
    for r in range(groups):
        for l in range(listed):
            slot = slot_ref[list_ref[r, l]]
            owner[r, l], local[r, l] = slot // slots, slot % slots
            live[r, l] = l < count_ref[r]
            at = jnp.where(live[r, l] & (owner[r, l] == r), local[r, l], -1)
            plan_ref[r, 2 * most + l] = at
        for lane in range(2 * most):
            plan_ref[r, lane] = jnp.int32(-1)
    low[0] = jnp.int32(most)
    for way in range(2):
        for lane in range(most):
            free[lane] = jnp.int32(most - 1 - lane)
        top[0] = jnp.int32(most)
        order = range(groups) if way == 0 else range(groups - 1, -1, -1)
        for z in order:
            for l in range(listed):
                behind = owner[z, l] < z if way == 0 else owner[z, l] > z

                @pl.when(live[z, l] & behind)
                def _():
                    lane = colour[z * listed + l]
                    plan_ref[z, 2 * most + l] = slots + way * most + lane
                    free[top[0]] = lane
                    top[0] = top[0] + 1

            for r in range(z + 1, groups) if way == 0 else range(z):
                for l in range(listed):

                    @pl.when(live[r, l] & (owner[r, l] == z))
                    def _():
                        top[0] = top[0] - 1
                        lane = free[top[0]]
                        colour[r * listed + l] = lane
                        plan_ref[z, way * most + lane] = local[r, l]
            low[0] = jnp.minimum(low[0], top[0])
    level = jnp.int32(0)
    for lanes in LEVELS:
        level = level + (most - low[0] > lanes).astype(jnp.int32)
    level_ref[0] = level


def plan(groups, slots, block_list, block_count, block_slot):
    listed = block_list.shape[1]
    most = most_flows(groups, listed)
    hbm = pl.BlockSpec(memory_space=pltpu.HBM)
    smem = pl.BlockSpec(memory_space=pltpu.SMEM)
    return pl.pallas_call(
        functools.partial(plan_kernel, groups, slots, most),
        name="plan",
        out_shape=(
            jax.ShapeDtypeStruct((groups, 2 * most + listed), jnp.int32),
            jax.ShapeDtypeStruct((1,), jnp.int32),
        ),
        in_specs=[hbm] * 3,
        out_specs=(smem, smem),
        scratch_shapes=table_scratch(block_list, block_count, block_slot) + [
            pltpu.SMEM((groups * listed,), jnp.int32),
            pltpu.SMEM((most + 1,), jnp.int32),
            pltpu.SMEM((1,), jnp.int32),
            pltpu.SMEM((1,), jnp.int32),
        ],
        compiler_params=pltpu.CompilerParams(vmem_limit_bytes=VMEM_BYTES),
    )(block_list, block_count, block_slot)


def exchange_kernel(
    groups, lanes, most, plan_ref, tiles_hbm, amp_ref, all_ref, weight_ref,
    tiles_ref, out_r, out_l, in_l, in_r, own_sem, tile_sem,
    r_send, r_recv, l_send, l_recv, a_send, a_recv,
):
    z = lax.axis_index("grp")
    m = lax.axis_index("mem")
    c, x, y = m % 2, (m // 2) % 2, m // 4
    sib = (y * 2 + x) * 2 + (1 - c)
    xn = (y * 2 + (1 - x)) * 2 + c
    yn = ((1 - y) * 2 + x) * 2 + c
    dg = ((1 - y) * 2 + (1 - x)) * 2 + c
    last = groups - 1
    after, before = lax.rem(z + 1, groups), lax.rem(z + groups - 1, groups)
    slots, tile_rows = tiles_hbm.shape[0], tiles_hbm.shape[1]
    listed = weight_ref.shape[0] // tile_rows
    occ, rows = amp_ref.shape[0], amp_ref.shape[1]
    part = rows // CHUNKS
    pieces = [(i, h) for h in range(CHUNKS) for i in range(occ)]

    tile_copy = pltpu.make_async_copy(tiles_hbm, tiles_ref, tile_sem)
    tile_copy.start()
    own = pltpu.make_async_copy(
        amp_ref, all_ref.at[:, pl.ds(pl.multiple_of(m * rows, 16), rows)], own_sem
    )
    own.start()
    barrier = pltpu.get_barrier_semaphore()

    def greet(device):
        pl.semaphore_signal(barrier, inc=1, device_id=device, device_id_type=MESH)

    for member in (sib, xn, yn):
        greet((z, member))

    @pl.when(z > 0)
    def _():
        greet((before, m))

    @pl.when(z < last)
    def _():
        greet((after, m))

    pl.semaphore_wait(barrier, 3 + (z + last) // groups + 1 - (z + 1) // groups)

    def block(owner, piece):
        i, h = piece
        return all_ref.at[i, pl.ds(pl.multiple_of(owner * rows + h * part, 16), part)]

    copies = []

    def send(kind, k, source, owner, target):
        copy = pltpu.make_async_remote_copy(
            source, block(owner, pieces[k]),
            a_send.at[kind, k], a_recv.at[kind, k],
            device_id=(z, target), device_id_type=MESH,
        )
        copy.start()
        copies.append(copy)
        return copy

    high = tile_rows // PIECES
    steps = lanes * PIECES

    def lane_copy(way, j):
        s, span = j // PIECES, pl.ds((j % PIECES) * high, high)
        source, target, ss, rs, to = (
            (out_r, in_l, r_send, r_recv, after), (out_l, in_r, l_send, l_recv, before)
        )[way]
        return pltpu.make_async_remote_copy(
            source.at[s, span], target.at[s, span], ss.at[j], rs.at[j],
            device_id=(to, m), device_id_type=MESH,
        )

    right = [lane_copy(0, j) for j in range(steps)]
    left = [lane_copy(1, j) for j in range(steps)]

    def lane_step(way, j):
        s, span = j // PIECES, pl.ds((j % PIECES) * high, high)
        code = plan_ref[z, way * most + s]
        outbox, inbox, copy = ((out_r, in_l, right), (out_l, in_r, left))[way]
        first, through = ((z == 0, (z > 0) & (z < last)), (z == last, (z > 0) & (z < last)))[way]

        @pl.when(first)
        def _():
            outbox[s, span] = tiles_ref[jnp.maximum(code, 0), span]
            copy[j].start()

        @pl.when(through)
        def _():
            copy[j].wait_recv()
            outbox[s, span] = lax.select(
                code >= 0, tiles_ref[jnp.maximum(code, 0), span], inbox[s, span]
            )
            copy[j].start()

    count = len(pieces)
    from_x, from_y, from_dg = [], [], []
    mine = [amp_ref.at[i, pl.ds(h * part, part)] for i, h in pieces]
    for k in range(count):
        from_x.append(send(0, k, mine[k], m, xn))
        from_y.append(send(1, k, mine[k], m, yn))
    tile_copy.wait()
    lane_step(0, 0)
    lane_step(1, 0)
    for k in range(count):
        send(2, k, mine[k], m, sib)
    for j in range(max(steps - 1, 2 * count)):
        if j < count:
            from_x[j].wait_recv()
            if j % 2 == 0:
                from_dg.append(send(3, j, block(xn, pieces[j]), xn, yn))
            send(4, j, block(xn, pieces[j]), xn, sib)
            from_y[j].wait_recv()
            if j % 2 == 1:
                from_dg.append(send(3, j, block(yn, pieces[j]), yn, xn))
            send(5, j, block(yn, pieces[j]), yn, sib)
        elif j < 2 * count:
            k = j - count
            from_dg[k].wait_recv()
            send(6, k, block(dg, pieces[k]), dg, sib)
        if j + 1 < steps:
            lane_step(0, j + 1)
            lane_step(1, j + 1)

    @pl.when(z == last)
    def _():
        for copy in right:
            copy.wait_recv()

    @pl.when(z == 0)
    def _():
        for copy in left:
            copy.wait_recv()

    for l in range(listed):
        code = plan_ref[z, 2 * most + l]
        held = tiles_ref[jnp.clip(code, 0, slots - 1)]
        by_right = in_l[jnp.clip(code - slots, 0, lanes - 1)]
        by_left = in_r[jnp.clip(code - slots - most, 0, lanes - 1)]
        tile = lax.select(
            code >= slots + most, by_left, lax.select(code >= slots, by_right, held)
        )
        weight_ref[l * tile_rows : (l + 1) * tile_rows] = lax.select(
            code >= 0, tile, jnp.zeros_like(tile)
        )

    waited = {id(copy) for copy in from_x + from_y + from_dg}
    own.wait()
    for copy in copies:
        if id(copy) not in waited:
            copy.wait_recv()
    for copy in copies:
        copy.wait_send()

    @pl.when(z < last)
    def _():
        for copy in right:
            copy.wait_send()

    @pl.when(z > 0)
    def _():
        for copy in left:
            copy.wait_send()


def exchange(number, lanes, listed, amplitudes, integrals, planned):
    groups, members = lax.axis_size("grp"), lax.axis_size("mem")
    occ, rows, depth = amplitudes.shape
    slots, tile_rows, columns = integrals.shape
    most = most_flows(groups, listed)
    count = occ * CHUNKS
    hbm = pl.BlockSpec(memory_space=pltpu.HBM)
    box = pltpu.VMEM((lanes, tile_rows, columns), integrals.dtype)
    lane_sems = pltpu.SemaphoreType.DMA((lanes * PIECES,))
    return pl.pallas_call(
        functools.partial(exchange_kernel, groups, lanes, most),
        name="exchange" + str(lanes),
        out_shape=(
            jax.ShapeDtypeStruct((occ, rows * members, depth), amplitudes.dtype),
            jax.ShapeDtypeStruct((listed * tile_rows, columns), integrals.dtype),
        ),
        in_specs=[pl.BlockSpec(memory_space=pltpu.SMEM), hbm, hbm],
        out_specs=(hbm, pl.BlockSpec(memory_space=pltpu.VMEM)),
        scratch_shapes=[
            pltpu.VMEM(integrals.shape, integrals.dtype), box, box, box, box,
            pltpu.SemaphoreType.DMA, pltpu.SemaphoreType.DMA,
            lane_sems, lane_sems, lane_sems, lane_sems,
            pltpu.SemaphoreType.DMA((7, count)),
            pltpu.SemaphoreType.DMA((7, count)),
        ],
        compiler_params=pltpu.CompilerParams(
            collective_id=number, has_side_effects=True, vmem_limit_bytes=VMEM_BYTES
        ),
    )(planned, integrals, amplitudes)


def product_kernel(step, amp_hbm, weight_hbm, out_ref, amp, weights, made, sem, amp_sem, out_sem):
    occ, rows, depth = amp_hbm.shape
    buffers, held, per = made.shape[0], amp.shape[0], rows // step
    total = occ * per
    load = pltpu.make_async_copy(weight_hbm, weights, sem)
    load.start()

    def fetch(t):
        return pltpu.make_async_copy(
            amp_hbm.at[t // per, pl.ds((t % per) * step, step)],
            amp.at[t % held], amp_sem.at[t % held],
        )

    def put(t):
        return pltpu.make_async_copy(
            made.at[t % buffers],
            out_ref.at[t // per, pl.ds((t % per) * step, step)],
            out_sem.at[t % buffers],
        )

    for t in range(held):
        fetch(t).start()
    load.wait()
    for t in range(total):
        fetch(t).wait()
        if t >= buffers:
            put(t - buffers).wait()
        made[t % buffers] = jnp.dot(
            amp[t % held], weights[...], preferred_element_type=jnp.float32
        )
        put(t).start()
        if t + held < total:
            fetch(t + held).start()
    for t in range(total - buffers, total):
        put(t).wait()


def product(amplitudes, weights):
    occ, rows, depth = amplitudes.shape
    columns = weights.shape[1]
    step = 256
    buffers = min(8, occ * rows // step)
    hbm = pl.BlockSpec(memory_space=pltpu.HBM)
    return pl.pallas_call(
        functools.partial(product_kernel, step),
        name="product",
        out_shape=jax.ShapeDtypeStruct((occ, rows, columns), jnp.float32),
        in_specs=[hbm] * 2,
        out_specs=hbm,
        scratch_shapes=[
            pltpu.VMEM((buffers, step, depth), amplitudes.dtype),
            pltpu.VMEM(weights.shape, weights.dtype),
            pltpu.VMEM((buffers, step, columns), jnp.float32),
            pltpu.SemaphoreType.DMA,
            pltpu.SemaphoreType.DMA((buffers,)),
            pltpu.SemaphoreType.DMA((buffers,)),
        ],
        compiler_params=pltpu.CompilerParams(vmem_limit_bytes=VMEM_BYTES),
    )(amplitudes, weights)


def planned_path(amplitudes, integrals, block_list, block_count, block_slot):
    groups = lax.axis_size("grp")
    listed = block_list.shape[1]
    most = most_flows(groups, listed)
    planned, level = plan(groups, integrals.shape[0], block_list, block_count, block_slot)
    sizes = LEVELS + (most,)
    branches = [
        functools.partial(exchange, number, lanes, listed) for number, lanes in enumerate(sizes)
    ]
    return lax.switch(level[0], branches, amplitudes, integrals, planned)


def gathered_path(amplitudes, integrals, block_list, block_count, block_slot):
    groups = lax.axis_size("grp")
    me = lax.axis_index("grp")
    listed = block_list.shape[1]
    slots, tile_rows, columns = integrals.shape
    table = block_slot[block_list]
    owner, local = table // slots, table % slots
    positions = jnp.arange(listed, dtype=jnp.int32)
    same = owner[:, :, None] == owner[:, None, :]
    same = same & (positions[None, None, :] < positions[None, :, None])
    rank = jnp.sum(same.astype(jnp.int32), axis=2)
    live = positions[None, :] < block_count[:, None]
    pick = (live & (owner == me))[:, None, :] & (
        rank[:, None, :] == jnp.arange(CAP, dtype=jnp.int32)[None, :, None]
    )
    sent = jnp.sum(jnp.where(pick, local[:, None, :], 0), axis=2)
    outgoing = integrals[sent.reshape(-1)].reshape(groups, CAP, tile_rows, columns)
    incoming = lax.all_to_all(outgoing, "grp", split_axis=0, concat_axis=0, tiled=True)
    incoming = incoming.reshape(groups * CAP, tile_rows, columns)
    chosen = incoming[owner[me] * CAP + jnp.minimum(rank[me], CAP - 1)]
    weights = jnp.where(live[me][:, None, None], chosen, jnp.zeros_like(chosen))
    weights = weights.reshape(listed * tile_rows, columns)
    return lax.all_gather(amplitudes, "mem", axis=1, tiled=True), weights


def per_device(by_plan, amplitudes, integrals, block_list, block_count, block_slot):
    move = planned_path if by_plan else gathered_path
    return product(*move(amplitudes, integrals, block_list, block_count, block_slot))


def solution(mesh):
    in_specs = (P("grp", "mem", None), P("grp", None, "mem"), P(), P(), P())
    out_specs = P("grp", None, "mem")
    by_plan = mesh.shape["mem"] == 8 and mesh.shape["grp"] == 4
    return jax.shard_map(
        functools.partial(per_device, by_plan), mesh=mesh,
        in_specs=in_specs, out_specs=out_specs, check_vma=False,
    )
```

```python
import functools

import jax
import jax.numpy as jnp
from jax import lax
from jax.experimental import pallas as pl
from jax.experimental.pallas import tpu as pltpu
from jax.sharding import PartitionSpec as P

CAP = 2
MESH = pl.DeviceIdType.MESH
CHUNKS = 2
PIECES = 2
LEVELS = (2, 3, 4, 5)
VMEM_BYTES = 60 * 2**20


def load_tables(sources, targets, sem):
    copies = [
        pltpu.make_async_copy(source, target, sem.at[k])
        for k, (source, target) in enumerate(zip(sources, targets))
    ]
    for copy in copies:
        copy.start()
    return copies


def table_scratch(block_list, block_count, block_slot):
    tables = (block_list, block_count, block_slot)
    return [pltpu.SMEM(t.shape, t.dtype) for t in tables] + [pltpu.SemaphoreType.DMA((3,))]


def most_flows(groups, listed):
    return max((groups - 1 - k) * min(listed, CAP * (k + 1)) for k in range(groups - 1))


def plan_kernel(
    groups, slots, most, list_hbm, count_hbm, slot_hbm, plan_ref, level_ref,
    list_ref, count_ref, slot_ref, table_sem, colour, free, top, low,
):
    listed = list_hbm.shape[1]
    for copy in load_tables(
        (list_hbm, count_hbm, slot_hbm), (list_ref, count_ref, slot_ref), table_sem
    ):
        copy.wait()
    owner, local, live = {}, {}, {}
    for r in range(groups):
        for l in range(listed):
            slot = slot_ref[list_ref[r, l]]
            owner[r, l], local[r, l] = slot // slots, slot % slots
            live[r, l] = l < count_ref[r]
            at = jnp.where(live[r, l] & (owner[r, l] == r), local[r, l], -1)
            plan_ref[r, 2 * most + l] = at
        for lane in range(2 * most):
            plan_ref[r, lane] = jnp.int32(-1)
    low[0] = jnp.int32(most)
    for way in range(2):
        for lane in range(most):
            free[lane] = jnp.int32(most - 1 - lane)
        top[0] = jnp.int32(most)
        order = range(groups) if way == 0 else range(groups - 1, -1, -1)
        for z in order:
            for l in range(listed):
                behind = owner[z, l] < z if way == 0 else owner[z, l] > z

                @pl.when(live[z, l] & behind)
                def _():
                    lane = colour[z * listed + l]
                    plan_ref[z, 2 * most + l] = slots + way * most + lane
                    free[top[0]] = lane
                    top[0] = top[0] + 1

            for r in range(z + 1, groups) if way == 0 else range(z):
                for l in range(listed):

                    @pl.when(live[r, l] & (owner[r, l] == z))
                    def _():
                        top[0] = top[0] - 1
                        lane = free[top[0]]
                        colour[r * listed + l] = lane
                        plan_ref[z, way * most + lane] = local[r, l]
            low[0] = jnp.minimum(low[0], top[0])
    level = jnp.int32(0)
    for lanes in LEVELS:
        level = level + (most - low[0] > lanes).astype(jnp.int32)
    level_ref[0] = level


def plan(groups, slots, block_list, block_count, block_slot):
    listed = block_list.shape[1]
    most = most_flows(groups, listed)
    hbm = pl.BlockSpec(memory_space=pltpu.HBM)
    smem = pl.BlockSpec(memory_space=pltpu.SMEM)
    return pl.pallas_call(
        functools.partial(plan_kernel, groups, slots, most),
        name="plan",
        out_shape=(
            jax.ShapeDtypeStruct((groups, 2 * most + listed), jnp.int32),
            jax.ShapeDtypeStruct((1,), jnp.int32),
        ),
        in_specs=[hbm] * 3,
        out_specs=(smem, smem),
        scratch_shapes=table_scratch(block_list, block_count, block_slot) + [
            pltpu.SMEM((groups * listed,), jnp.int32),
            pltpu.SMEM((most + 1,), jnp.int32),
            pltpu.SMEM((1,), jnp.int32),
            pltpu.SMEM((1,), jnp.int32),
        ],
        compiler_params=pltpu.CompilerParams(vmem_limit_bytes=VMEM_BYTES),
    )(block_list, block_count, block_slot)


def exchange_kernel(
    groups, lanes, most, plan_ref, tiles_hbm, amp_ref, all_ref, weight_ref,
    tiles_ref, out_r, out_l, in_l, in_r, own_sem, tile_sem,
    r_send, r_recv, l_send, l_recv, a_send, a_recv,
):
    z = lax.axis_index("grp")
    m = lax.axis_index("mem")
    c, x, y = m % 2, (m // 2) % 2, m // 4
    sib = (y * 2 + x) * 2 + (1 - c)
    xn = (y * 2 + (1 - x)) * 2 + c
    yn = ((1 - y) * 2 + x) * 2 + c
    dg = ((1 - y) * 2 + (1 - x)) * 2 + c
    last = groups - 1
    after, before = lax.rem(z + 1, groups), lax.rem(z + groups - 1, groups)
    slots, tile_rows = tiles_hbm.shape[0], tiles_hbm.shape[1]
    listed = weight_ref.shape[0] // tile_rows
    occ, rows = amp_ref.shape[0], amp_ref.shape[1]
    part = rows // CHUNKS
    pieces = [(i, h) for h in range(CHUNKS) for i in range(occ)]

    tile_copy = pltpu.make_async_copy(tiles_hbm, tiles_ref, tile_sem)
    tile_copy.start()
    own = pltpu.make_async_copy(
        amp_ref, all_ref.at[:, pl.ds(pl.multiple_of(m * rows, 16), rows)], own_sem
    )
    own.start()
    barrier = pltpu.get_barrier_semaphore()

    def greet(device):
        pl.semaphore_signal(barrier, inc=1, device_id=device, device_id_type=MESH)

    for member in (sib, xn, yn):
        greet((z, member))

    @pl.when(z > 0)
    def _():
        greet((before, m))

    @pl.when(z < last)
    def _():
        greet((after, m))

    pl.semaphore_wait(barrier, 3 + (z + last) // groups + 1 - (z + 1) // groups)

    def block(owner, piece):
        i, h = piece
        return all_ref.at[i, pl.ds(pl.multiple_of(owner * rows + h * part, 16), part)]

    copies = []

    def send(kind, k, source, owner, target):
        copy = pltpu.make_async_remote_copy(
            source, block(owner, pieces[k]),
            a_send.at[kind, k], a_recv.at[kind, k],
            device_id=(z, target), device_id_type=MESH,
        )
        copy.start()
        copies.append(copy)
        return copy

    high = tile_rows // PIECES
    steps = lanes * PIECES

    def lane_copy(way, j):
        s, span = j // PIECES, pl.ds((j % PIECES) * high, high)
        source, target, ss, rs, to = (
            (out_r, in_l, r_send, r_recv, after), (out_l, in_r, l_send, l_recv, before)
        )[way]
        return pltpu.make_async_remote_copy(
            source.at[s, span], target.at[s, span], ss.at[j], rs.at[j],
            device_id=(to, m), device_id_type=MESH,
        )

    right = [lane_copy(0, j) for j in range(steps)]
    left = [lane_copy(1, j) for j in range(steps)]

    def lane_step(way, j):
        s, span = j // PIECES, pl.ds((j % PIECES) * high, high)
        code = plan_ref[z, way * most + s]
        outbox, inbox, copy = ((out_r, in_l, right), (out_l, in_r, left))[way]
        first, through = ((z == 0, (z > 0) & (z < last)), (z == last, (z > 0) & (z < last)))[way]

        @pl.when(first)
        def _():
            outbox[s, span] = tiles_ref[jnp.maximum(code, 0), span]
            copy[j].start()

        @pl.when(through)
        def _():
            copy[j].wait_recv()
            outbox[s, span] = lax.select(
                code >= 0, tiles_ref[jnp.maximum(code, 0), span], inbox[s, span]
            )
            copy[j].start()

    count = len(pieces)
    from_x, from_y, from_dg = [], [], []
    mine = [amp_ref.at[i, pl.ds(h * part, part)] for i, h in pieces]
    for k in range(count):
        from_x.append(send(0, k, mine[k], m, xn))
        from_y.append(send(1, k, mine[k], m, yn))
    tile_copy.wait()
    lane_step(0, 0)
    lane_step(1, 0)
    for k in range(count):
        send(2, k, mine[k], m, sib)
    for j in range(max(steps - 1, 2 * count)):
        if j < count:
            from_x[j].wait_recv()
            if j % 2 == 0:
                from_dg.append(send(3, j, block(xn, pieces[j]), xn, yn))
            send(4, j, block(xn, pieces[j]), xn, sib)
            from_y[j].wait_recv()
            if j % 2 == 1:
                from_dg.append(send(3, j, block(yn, pieces[j]), yn, xn))
            send(5, j, block(yn, pieces[j]), yn, sib)
        elif j < 2 * count:
            k = j - count
            from_dg[k].wait_recv()
            send(6, k, block(dg, pieces[k]), dg, sib)
        if j + 1 < steps:
            lane_step(0, j + 1)
            lane_step(1, j + 1)

    @pl.when(z == last)
    def _():
        for copy in right:
            copy.wait_recv()

    @pl.when(z == 0)
    def _():
        for copy in left:
            copy.wait_recv()

    for l in range(listed):
        code = plan_ref[z, 2 * most + l]
        held = tiles_ref[jnp.clip(code, 0, slots - 1)]
        by_right = in_l[jnp.clip(code - slots, 0, lanes - 1)]
        by_left = in_r[jnp.clip(code - slots - most, 0, lanes - 1)]
        tile = lax.select(
            code >= slots + most, by_left, lax.select(code >= slots, by_right, held)
        )
        weight_ref[l * tile_rows : (l + 1) * tile_rows] = lax.select(
            code >= 0, tile, jnp.zeros_like(tile)
        )

    waited = {id(copy) for copy in from_x + from_y + from_dg}
    own.wait()
    for copy in copies:
        if id(copy) not in waited:
            copy.wait_recv()
    for copy in copies:
        copy.wait_send()

    @pl.when(z < last)
    def _():
        for copy in right:
            copy.wait_send()

    @pl.when(z > 0)
    def _():
        for copy in left:
            copy.wait_send()


def exchange(number, lanes, listed, amplitudes, integrals, planned):
    groups, members = lax.axis_size("grp"), lax.axis_size("mem")
    occ, rows, depth = amplitudes.shape
    slots, tile_rows, columns = integrals.shape
    most = most_flows(groups, listed)
    count = occ * CHUNKS
    hbm = pl.BlockSpec(memory_space=pltpu.HBM)
    vmem = pl.BlockSpec(memory_space=pltpu.VMEM)
    box = pltpu.VMEM((lanes, tile_rows, columns), integrals.dtype)
    lane_sems = pltpu.SemaphoreType.DMA((lanes * PIECES,))
    return pl.pallas_call(
        functools.partial(exchange_kernel, groups, lanes, most),
        name="exchange" + str(lanes),
        out_shape=(
            jax.ShapeDtypeStruct((occ, rows * members, depth), amplitudes.dtype),
            jax.ShapeDtypeStruct((listed * tile_rows, columns), integrals.dtype),
        ),
        in_specs=[pl.BlockSpec(memory_space=pltpu.SMEM), hbm, vmem],
        out_specs=(vmem, vmem),
        scratch_shapes=[
            pltpu.VMEM(integrals.shape, integrals.dtype), box, box, box, box,
            pltpu.SemaphoreType.DMA, pltpu.SemaphoreType.DMA,
            lane_sems, lane_sems, lane_sems, lane_sems,
            pltpu.SemaphoreType.DMA((7, count)),
            pltpu.SemaphoreType.DMA((7, count)),
        ],
        compiler_params=pltpu.CompilerParams(
            collective_id=number, has_side_effects=True, vmem_limit_bytes=VMEM_BYTES
        ),
    )(planned, integrals, amplitudes)


def product_kernel(step, amp_hbm, weight_hbm, out_ref, amp, weights, made, sem, amp_sem, out_sem):
    occ, rows, depth = amp_hbm.shape
    buffers, held, per = made.shape[0], amp.shape[0], rows // step
    total = occ * per
    load = pltpu.make_async_copy(weight_hbm, weights, sem)
    load.start()

    def fetch(t):
        return pltpu.make_async_copy(
            amp_hbm.at[t // per, pl.ds((t % per) * step, step)],
            amp.at[t % held], amp_sem.at[t % held],
        )

    def put(t):
        return pltpu.make_async_copy(
            made.at[t % buffers],
            out_ref.at[t // per, pl.ds((t % per) * step, step)],
            out_sem.at[t % buffers],
        )

    for t in range(held):
        fetch(t).start()
    load.wait()
    for t in range(total):
        fetch(t).wait()
        if t >= buffers:
            put(t - buffers).wait()
        made[t % buffers] = jnp.dot(
            amp[t % held], weights[...], preferred_element_type=jnp.float32
        )
        put(t).start()
        if t + held < total:
            fetch(t + held).start()
    for t in range(total - buffers, total):
        put(t).wait()


def product(amplitudes, weights):
    occ, rows, depth = amplitudes.shape
    columns = weights.shape[1]
    step = 256
    buffers = min(8, occ * rows // step)
    hbm = pl.BlockSpec(memory_space=pltpu.HBM)
    return pl.pallas_call(
        functools.partial(product_kernel, step),
        name="product",
        out_shape=jax.ShapeDtypeStruct((occ, rows, columns), jnp.float32),
        in_specs=[hbm] * 2,
        out_specs=hbm,
        scratch_shapes=[
            pltpu.VMEM((buffers, step, depth), amplitudes.dtype),
            pltpu.VMEM(weights.shape, weights.dtype),
            pltpu.VMEM((buffers, step, columns), jnp.float32),
            pltpu.SemaphoreType.DMA,
            pltpu.SemaphoreType.DMA((buffers,)),
            pltpu.SemaphoreType.DMA((buffers,)),
        ],
        compiler_params=pltpu.CompilerParams(vmem_limit_bytes=VMEM_BYTES),
    )(amplitudes, weights)


def planned_path(amplitudes, integrals, block_list, block_count, block_slot):
    groups = lax.axis_size("grp")
    listed = block_list.shape[1]
    most = most_flows(groups, listed)
    planned, level = plan(groups, integrals.shape[0], block_list, block_count, block_slot)
    sizes = LEVELS + (most,)
    branches = [
        functools.partial(exchange, number, lanes, listed) for number, lanes in enumerate(sizes)
    ]
    return lax.switch(level[0], branches, amplitudes, integrals, planned)


def gathered_path(amplitudes, integrals, block_list, block_count, block_slot):
    groups = lax.axis_size("grp")
    me = lax.axis_index("grp")
    listed = block_list.shape[1]
    slots, tile_rows, columns = integrals.shape
    table = block_slot[block_list]
    owner, local = table // slots, table % slots
    positions = jnp.arange(listed, dtype=jnp.int32)
    same = owner[:, :, None] == owner[:, None, :]
    same = same & (positions[None, None, :] < positions[None, :, None])
    rank = jnp.sum(same.astype(jnp.int32), axis=2)
    live = positions[None, :] < block_count[:, None]
    pick = (live & (owner == me))[:, None, :] & (
        rank[:, None, :] == jnp.arange(CAP, dtype=jnp.int32)[None, :, None]
    )
    sent = jnp.sum(jnp.where(pick, local[:, None, :], 0), axis=2)
    outgoing = integrals[sent.reshape(-1)].reshape(groups, CAP, tile_rows, columns)
    incoming = lax.all_to_all(outgoing, "grp", split_axis=0, concat_axis=0, tiled=True)
    incoming = incoming.reshape(groups * CAP, tile_rows, columns)
    chosen = incoming[owner[me] * CAP + jnp.minimum(rank[me], CAP - 1)]
    weights = jnp.where(live[me][:, None, None], chosen, jnp.zeros_like(chosen))
    weights = weights.reshape(listed * tile_rows, columns)
    return lax.all_gather(amplitudes, "mem", axis=1, tiled=True), weights


def per_device(by_plan, amplitudes, integrals, block_list, block_count, block_slot):
    move = planned_path if by_plan else gathered_path
    return product(*move(amplitudes, integrals, block_list, block_count, block_slot))


def solution(mesh):
    in_specs = (P("grp", "mem", None), P("grp", None, "mem"), P(), P(), P())
    out_specs = P("grp", None, "mem")
    by_plan = mesh.shape["mem"] == 8 and mesh.shape["grp"] == 4
    return jax.shard_map(
        functools.partial(per_device, by_plan), mesh=mesh,
        in_specs=in_specs, out_specs=out_specs, check_vma=False,
    )
```

```python
import functools

import jax
import jax.numpy as jnp
from jax import lax
from jax.experimental import pallas as pl
from jax.experimental.pallas import tpu as pltpu
from jax.sharding import PartitionSpec as P

CAP = 2
MESH = pl.DeviceIdType.MESH
CHUNKS = 2
PIECES = 2
LEAD = 2
LEVELS = (2, 3, 4, 5)
VMEM_BYTES = 60 * 2**20


def load_tables(sources, targets, sem):
    copies = [
        pltpu.make_async_copy(source, target, sem.at[k])
        for k, (source, target) in enumerate(zip(sources, targets))
    ]
    for copy in copies:
        copy.start()
    return copies


def table_scratch(block_list, block_count, block_slot):
    tables = (block_list, block_count, block_slot)
    return [pltpu.SMEM(t.shape, t.dtype) for t in tables] + [pltpu.SemaphoreType.DMA((3,))]


def most_flows(groups, listed):
    return max((groups - 1 - k) * min(listed, CAP * (k + 1)) for k in range(groups - 1))


def plan_kernel(
    groups, slots, most, list_hbm, count_hbm, slot_hbm, plan_ref, level_ref,
    list_ref, count_ref, slot_ref, table_sem, colour, free, top, low,
):
    listed = list_hbm.shape[1]
    for copy in load_tables(
        (list_hbm, count_hbm, slot_hbm), (list_ref, count_ref, slot_ref), table_sem
    ):
        copy.wait()
    owner, local, live = {}, {}, {}
    for r in range(groups):
        for l in range(listed):
            slot = slot_ref[list_ref[r, l]]
            owner[r, l], local[r, l] = slot // slots, slot % slots
            live[r, l] = l < count_ref[r]
            at = jnp.where(live[r, l] & (owner[r, l] == r), local[r, l], -1)
            plan_ref[r, 2 * most + l] = at
        for lane in range(2 * most):
            plan_ref[r, lane] = jnp.int32(-1)
    low[0] = jnp.int32(most)
    for way in range(2):
        for lane in range(most):
            free[lane] = jnp.int32(most - 1 - lane)
        top[0] = jnp.int32(most)
        order = range(groups) if way == 0 else range(groups - 1, -1, -1)
        for z in order:
            for l in range(listed):
                behind = owner[z, l] < z if way == 0 else owner[z, l] > z

                @pl.when(live[z, l] & behind)
                def _():
                    lane = colour[z * listed + l]
                    plan_ref[z, 2 * most + l] = slots + way * most + lane
                    free[top[0]] = lane
                    top[0] = top[0] + 1

            for r in range(z + 1, groups) if way == 0 else range(z):
                for l in range(listed):

                    @pl.when(live[r, l] & (owner[r, l] == z))
                    def _():
                        top[0] = top[0] - 1
                        lane = free[top[0]]
                        colour[r * listed + l] = lane
                        plan_ref[z, way * most + lane] = local[r, l]
            low[0] = jnp.minimum(low[0], top[0])
    level = jnp.int32(0)
    for lanes in LEVELS:
        level = level + (most - low[0] > lanes).astype(jnp.int32)
    level_ref[0] = level


def plan(groups, slots, block_list, block_count, block_slot):
    listed = block_list.shape[1]
    most = most_flows(groups, listed)
    hbm = pl.BlockSpec(memory_space=pltpu.HBM)
    smem = pl.BlockSpec(memory_space=pltpu.SMEM)
    return pl.pallas_call(
        functools.partial(plan_kernel, groups, slots, most),
        name="plan",
        out_shape=(
            jax.ShapeDtypeStruct((groups, 2 * most + listed), jnp.int32),
            jax.ShapeDtypeStruct((1,), jnp.int32),
        ),
        in_specs=[hbm] * 3,
        out_specs=(smem, smem),
        scratch_shapes=table_scratch(block_list, block_count, block_slot) + [
            pltpu.SMEM((groups * listed,), jnp.int32),
            pltpu.SMEM((most + 1,), jnp.int32),
            pltpu.SMEM((1,), jnp.int32),
            pltpu.SMEM((1,), jnp.int32),
        ],
        compiler_params=pltpu.CompilerParams(vmem_limit_bytes=VMEM_BYTES),
    )(block_list, block_count, block_slot)


def exchange_kernel(
    groups, lanes, most, plan_ref, tiles_hbm, amp_ref, all_ref, weight_ref,
    tiles_ref, out_r, out_l, in_l, in_r, own_sem, tile_sem,
    r_send, r_recv, l_send, l_recv, a_send, a_recv,
):
    z = lax.axis_index("grp")
    m = lax.axis_index("mem")
    c, x, y = m % 2, (m // 2) % 2, m // 4
    sib = (y * 2 + x) * 2 + (1 - c)
    xn = (y * 2 + (1 - x)) * 2 + c
    yn = ((1 - y) * 2 + x) * 2 + c
    dg = ((1 - y) * 2 + (1 - x)) * 2 + c
    last = groups - 1
    after, before = lax.rem(z + 1, groups), lax.rem(z + groups - 1, groups)
    slots, tile_rows = tiles_hbm.shape[0], tiles_hbm.shape[1]
    listed = weight_ref.shape[0] // tile_rows
    occ, rows = amp_ref.shape[0], amp_ref.shape[1]
    part = rows // CHUNKS
    pieces = [(i, h) for h in range(CHUNKS) for i in range(occ)]

    tile_copy = pltpu.make_async_copy(tiles_hbm, tiles_ref, tile_sem)
    tile_copy.start()
    own = pltpu.make_async_copy(
        amp_ref, all_ref.at[:, pl.ds(pl.multiple_of(m * rows, 16), rows)], own_sem
    )
    own.start()
    barrier = pltpu.get_barrier_semaphore()

    def greet(device):
        pl.semaphore_signal(barrier, inc=1, device_id=device, device_id_type=MESH)

    for member in (sib, xn, yn):
        greet((z, member))

    @pl.when(z > 0)
    def _():
        greet((before, m))

    @pl.when(z < last)
    def _():
        greet((after, m))

    pl.semaphore_wait(barrier, 3 + (z + last) // groups + 1 - (z + 1) // groups)

    def block(owner, piece):
        i, h = piece
        return all_ref.at[i, pl.ds(pl.multiple_of(owner * rows + h * part, 16), part)]

    copies = []

    def send(kind, k, source, owner, target):
        copy = pltpu.make_async_remote_copy(
            source, block(owner, pieces[k]),
            a_send.at[kind, k], a_recv.at[kind, k],
            device_id=(z, target), device_id_type=MESH,
        )
        copy.start()
        copies.append(copy)
        return copy

    high = tile_rows // PIECES
    steps = lanes * PIECES

    def lane_copy(way, j):
        s, span = j // PIECES, pl.ds((j % PIECES) * high, high)
        source, target, ss, rs, to = (
            (out_r, in_l, r_send, r_recv, after), (out_l, in_r, l_send, l_recv, before)
        )[way]
        return pltpu.make_async_remote_copy(
            source.at[s, span], target.at[s, span], ss.at[j], rs.at[j],
            device_id=(to, m), device_id_type=MESH,
        )

    right = [lane_copy(0, j) for j in range(steps)]
    left = [lane_copy(1, j) for j in range(steps)]

    def lane_step(near, way, j):
        s, span = j // PIECES, pl.ds((j % PIECES) * high, high)
        code = plan_ref[z, way * most + s]
        outbox, inbox, copy = ((out_r, in_l, right), (out_l, in_r, left))[way]
        lower, upper = (z > 0) & (z < half), (z >= half) & (z < last)
        first = (z == 0, z == last)[way]
        through = lower if near == (way == 0) else upper

        if near:

            @pl.when(first)
            def _():
                outbox[s, span] = tiles_ref[jnp.maximum(code, 0), span]
                copy[j].start()

        @pl.when(through)
        def _():
            copy[j].wait_recv()
            outbox[s, span] = lax.select(
                code >= 0, tiles_ref[jnp.maximum(code, 0), span], inbox[s, span]
            )
            copy[j].start()

    half = groups // 2

    def lane_steps(j):
        if j < steps:
            lane_step(True, 0, j)
            lane_step(True, 1, j)
        if 0 <= j - LEAD < steps:
            lane_step(False, 0, j - LEAD)
            lane_step(False, 1, j - LEAD)

    count = len(pieces)
    from_x, from_y, from_dg = [], [], []
    mine = [amp_ref.at[i, pl.ds(h * part, part)] for i, h in pieces]
    for k in range(count):
        from_x.append(send(0, k, mine[k], m, xn))
        from_y.append(send(1, k, mine[k], m, yn))
    tile_copy.wait()
    lane_steps(0)
    for k in range(count):
        send(2, k, mine[k], m, sib)
    for j in range(max(steps - 1 + LEAD, 2 * count)):
        if j < count:
            from_x[j].wait_recv()
            if j % 2 == 0:
                from_dg.append(send(3, j, block(xn, pieces[j]), xn, yn))
            send(4, j, block(xn, pieces[j]), xn, sib)
            from_y[j].wait_recv()
            if j % 2 == 1:
                from_dg.append(send(3, j, block(yn, pieces[j]), yn, xn))
            send(5, j, block(yn, pieces[j]), yn, sib)
        elif j < 2 * count:
            k = j - count
            from_dg[k].wait_recv()
            send(6, k, block(dg, pieces[k]), dg, sib)
        lane_steps(j + 1)

    @pl.when(z == last)
    def _():
        for copy in right:
            copy.wait_recv()

    @pl.when(z == 0)
    def _():
        for copy in left:
            copy.wait_recv()

    for l in range(listed):
        code = plan_ref[z, 2 * most + l]
        held = tiles_ref[jnp.clip(code, 0, slots - 1)]
        by_right = in_l[jnp.clip(code - slots, 0, lanes - 1)]
        by_left = in_r[jnp.clip(code - slots - most, 0, lanes - 1)]
        tile = lax.select(
            code >= slots + most, by_left, lax.select(code >= slots, by_right, held)
        )
        weight_ref[l * tile_rows : (l + 1) * tile_rows] = lax.select(
            code >= 0, tile, jnp.zeros_like(tile)
        )

    waited = {id(copy) for copy in from_x + from_y + from_dg}
    own.wait()
    for copy in copies:
        if id(copy) not in waited:
            copy.wait_recv()
    for copy in copies:
        copy.wait_send()

    @pl.when(z < last)
    def _():
        for copy in right:
            copy.wait_send()

    @pl.when(z > 0)
    def _():
        for copy in left:
            copy.wait_send()


def exchange(number, lanes, listed, amplitudes, integrals, planned):
    groups, members = lax.axis_size("grp"), lax.axis_size("mem")
    occ, rows, depth = amplitudes.shape
    slots, tile_rows, columns = integrals.shape
    most = most_flows(groups, listed)
    count = occ * CHUNKS
    hbm = pl.BlockSpec(memory_space=pltpu.HBM)
    vmem = pl.BlockSpec(memory_space=pltpu.VMEM)
    box = pltpu.VMEM((lanes, tile_rows, columns), integrals.dtype)
    lane_sems = pltpu.SemaphoreType.DMA((lanes * PIECES,))
    return pl.pallas_call(
        functools.partial(exchange_kernel, groups, lanes, most),
        name="exchange" + str(lanes),
        out_shape=(
            jax.ShapeDtypeStruct((occ, rows * members, depth), amplitudes.dtype),
            jax.ShapeDtypeStruct((listed * tile_rows, columns), integrals.dtype),
        ),
        in_specs=[pl.BlockSpec(memory_space=pltpu.SMEM), hbm, vmem],
        out_specs=(vmem, vmem),
        scratch_shapes=[
            pltpu.VMEM(integrals.shape, integrals.dtype), box, box, box, box,
            pltpu.SemaphoreType.DMA, pltpu.SemaphoreType.DMA,
            lane_sems, lane_sems, lane_sems, lane_sems,
            pltpu.SemaphoreType.DMA((7, count)),
            pltpu.SemaphoreType.DMA((7, count)),
        ],
        compiler_params=pltpu.CompilerParams(
            collective_id=number, has_side_effects=True, vmem_limit_bytes=VMEM_BYTES
        ),
    )(planned, integrals, amplitudes)


def product_kernel(step, amp_hbm, weight_hbm, out_ref, amp, weights, made, sem, amp_sem, out_sem):
    occ, rows, depth = amp_hbm.shape
    buffers, held, per = made.shape[0], amp.shape[0], rows // step
    total = occ * per
    load = pltpu.make_async_copy(weight_hbm, weights, sem)
    load.start()

    def fetch(t):
        return pltpu.make_async_copy(
            amp_hbm.at[t // per, pl.ds((t % per) * step, step)],
            amp.at[t % held], amp_sem.at[t % held],
        )

    def put(t):
        return pltpu.make_async_copy(
            made.at[t % buffers],
            out_ref.at[t // per, pl.ds((t % per) * step, step)],
            out_sem.at[t % buffers],
        )

    for t in range(held):
        fetch(t).start()
    load.wait()
    for t in range(total):
        fetch(t).wait()
        if t >= buffers:
            put(t - buffers).wait()
        made[t % buffers] = jnp.dot(
            amp[t % held], weights[...], preferred_element_type=jnp.float32
        )
        put(t).start()
        if t + held < total:
            fetch(t + held).start()
    for t in range(total - buffers, total):
        put(t).wait()


def product(amplitudes, weights):
    occ, rows, depth = amplitudes.shape
    columns = weights.shape[1]
    step = 256
    buffers = min(8, occ * rows // step)
    hbm = pl.BlockSpec(memory_space=pltpu.HBM)
    return pl.pallas_call(
        functools.partial(product_kernel, step),
        name="product",
        out_shape=jax.ShapeDtypeStruct((occ, rows, columns), jnp.float32),
        in_specs=[hbm] * 2,
        out_specs=hbm,
        scratch_shapes=[
            pltpu.VMEM((buffers, step, depth), amplitudes.dtype),
            pltpu.VMEM(weights.shape, weights.dtype),
            pltpu.VMEM((buffers, step, columns), jnp.float32),
            pltpu.SemaphoreType.DMA,
            pltpu.SemaphoreType.DMA((buffers,)),
            pltpu.SemaphoreType.DMA((buffers,)),
        ],
        compiler_params=pltpu.CompilerParams(vmem_limit_bytes=VMEM_BYTES),
    )(amplitudes, weights)


def planned_path(amplitudes, integrals, block_list, block_count, block_slot):
    groups = lax.axis_size("grp")
    listed = block_list.shape[1]
    most = most_flows(groups, listed)
    planned, level = plan(groups, integrals.shape[0], block_list, block_count, block_slot)
    sizes = LEVELS + (most,)
    branches = [
        functools.partial(exchange, number, lanes, listed) for number, lanes in enumerate(sizes)
    ]
    return lax.switch(level[0], branches, amplitudes, integrals, planned)


def gathered_path(amplitudes, integrals, block_list, block_count, block_slot):
    groups = lax.axis_size("grp")
    me = lax.axis_index("grp")
    listed = block_list.shape[1]
    slots, tile_rows, columns = integrals.shape
    table = block_slot[block_list]
    owner, local = table // slots, table % slots
    positions = jnp.arange(listed, dtype=jnp.int32)
    same = owner[:, :, None] == owner[:, None, :]
    same = same & (positions[None, None, :] < positions[None, :, None])
    rank = jnp.sum(same.astype(jnp.int32), axis=2)
    live = positions[None, :] < block_count[:, None]
    pick = (live & (owner == me))[:, None, :] & (
        rank[:, None, :] == jnp.arange(CAP, dtype=jnp.int32)[None, :, None]
    )
    sent = jnp.sum(jnp.where(pick, local[:, None, :], 0), axis=2)
    outgoing = integrals[sent.reshape(-1)].reshape(groups, CAP, tile_rows, columns)
    incoming = lax.all_to_all(outgoing, "grp", split_axis=0, concat_axis=0, tiled=True)
    incoming = incoming.reshape(groups * CAP, tile_rows, columns)
    chosen = incoming[owner[me] * CAP + jnp.minimum(rank[me], CAP - 1)]
    weights = jnp.where(live[me][:, None, None], chosen, jnp.zeros_like(chosen))
    weights = weights.reshape(listed * tile_rows, columns)
    return lax.all_gather(amplitudes, "mem", axis=1, tiled=True), weights


def per_device(by_plan, amplitudes, integrals, block_list, block_count, block_slot):
    move = planned_path if by_plan else gathered_path
    return product(*move(amplitudes, integrals, block_list, block_count, block_slot))


def solution(mesh):
    in_specs = (P("grp", "mem", None), P("grp", None, "mem"), P(), P(), P())
    out_specs = P("grp", None, "mem")
    by_plan = mesh.shape["mem"] == 8 and mesh.shape["grp"] == 4
    return jax.shard_map(
        functools.partial(per_device, by_plan), mesh=mesh,
        in_specs=in_specs, out_specs=out_specs, check_vma=False,
    )
```
